128 devices in a mesh: tm: 16 (over x_lo, y, core), seq: 8 (over x_hi, z).
Axes of the slice: x: 4 (x_hi: 2, x_lo: 2; x = x_hi * 2 + x_lo), y: 4, z: 4, core: 2. Of those that a mesh axis runs over, the one named last changes fastest.
Arguments:
- states: float32 [16, 512, 5120], P('tm', 'seq'), may hold values from -6 to 6
- start: float32 [512, 5120], P('seq'), may hold values from -6 to 6
- t_index: int32 [16], P('tm'), may hold values from 0 to 49
- coef: float32 [50], replicated, may hold values from 0.05 to 0.5
- mod_table: float32 [50, 3, 5120], replicated, may hold values from -3 to 3
- wqkv: bfloat16 [3, 5120, 5120], P(None, 'tm', 'seq'), may hold values from -0.078125 to 0.078125
- wo: bfloat16 [5120, 5120], P('seq'), may hold values from -0.078125 to 0.078125
Outputs:
- new_states: float32 [16, 512, 5120], P('tm', 'seq')
The draws below stay inside these ranges and needn't reach their ends.
All inputs are finite; a program needn't handle non-finite values.
Results may differ from the reference program's by a relative error of at most 0.0023.
Values may be sent and summed in bfloat16 or wider, within the bound.
No kernel may reach another device: no remote copies, remote signals or barrier semaphores. Data moves between devices by JAX's collectives and lax.ppermute only.
A program may use at most 128 MiB of HBM per device.

```python
import math
import jax
import jax.numpy as jnp
from jax import lax

D = 5120
HEADS = 40
HEAD_DIM = 128
STEPS = 50
TOKENS = 512
WINDOW = 16


def plant(entries, key, low, largest):
    place = [jax.random.randint(jax.random.fold_in(key, axis), (), 0, length) for axis, length in enumerate(entries.shape)]
    longest = entries.shape.index(max(entries.shape))
    beside = place[:longest] + [(place[longest] + 1) % entries.shape[longest]] + place[longest + 1:]
    return entries.at[tuple(place)].set(low).at[tuple(beside)].set(largest)


def level_of(stream_key, shape, pieces, smallest, largest):
    factor_of, own = 1.0, jax.random.fold_in(stream_key, 6)
    for position, blocks in pieces:
        steps = jnp.exp(jax.random.uniform(jax.random.fold_in(own, position), (blocks,), jnp.float32, smallest / len(pieces), largest / len(pieces)))
        factor_of = factor_of * jnp.repeat(steps, shape[position] // blocks).reshape([-1 if axis == position else 1 for axis in range(len(shape))])
    return factor_of


def gaussian(rng, dims, scale, most, cuts=(), dtype=jnp.bfloat16):
    values = jax.random.normal(rng, dims, jnp.float32) * scale
    if len(cuts) > 0:
        values = level_of(rng, dims, cuts, -0.22, 0.18) * values
    return jnp.clip(values, min=-most, max=most).astype(dtype)


def setup_inputs(seed: int = 0) -> dict:
    arg_keys = jax.random.split(jax.random.key(seed), 8)
    return {
        "states": gaussian(arg_keys[0], (WINDOW, TOKENS, D), 1.0, 6.0, ((0, 16), (1, 8)), jnp.float32),
        "start": gaussian(arg_keys[1], (TOKENS, D), 1.0, 6.0, ((0, 8),), jnp.float32),
        "t_index": plant(jax.random.randint(arg_keys[2], (WINDOW,), 0, STEPS), jax.random.fold_in(arg_keys[2], 1), 0, STEPS - 1).astype(jnp.int32),
        "coef": jnp.clip(jnp.exp(jax.random.uniform(arg_keys[3], (STEPS,), jnp.float32, math.log(0.05), math.log(0.5))), 0.05, 0.5),
        "mod_table": gaussian(arg_keys[4], (STEPS, 3, D), 0.5, 3.0, (), jnp.float32),
        "wqkv": gaussian(arg_keys[5], (3, D, HEADS * HEAD_DIM), D ** -0.5, 0.078125, ((1, 16), (2, 8))),
        "wo": gaussian(arg_keys[6], (HEADS * HEAD_DIM, D), (HEADS * HEAD_DIM) ** -0.5, 0.078125, ((0, 8),)),
    }


def prepare(projected):
    count = projected.shape[1]
    per_head = projected.reshape(3, count, -1, HEAD_DIM)
    query_key = per_head[:2]
    query_key = query_key * lax.rsqrt(lax.optimization_barrier(jnp.mean(query_key * query_key, axis=-1, keepdims=True)) + 1e-06)
    return jnp.concatenate([query_key, per_head[2:]], axis=0).astype(jnp.bfloat16)

def drift_of(state, step_index, mod_table, wqkv, wo):
    modulation = jnp.take(mod_table, step_index, axis=0)
    shift_row, scale_row, gate_row = (modulation[0], modulation[1], modulation[2])
    center = lax.optimization_barrier(jnp.mean(state, axis=-1, keepdims=True))
    spread = lax.optimization_barrier(jnp.mean((state - center) * (state - center), axis=-1, keepdims=True))
    modded = ((state - center) * lax.rsqrt(spread + 1e-06) * (1.0 + scale_row) + shift_row).astype(jnp.bfloat16)
    projected = jnp.stack([jnp.dot(modded, wqkv[j], preferred_element_type=jnp.float32) for j in range(3)])
    prepared = prepare(projected)
    query = prepared[0].astype(jnp.float32)
    keys = prepared[1].astype(jnp.float32)
    values = prepared[2].astype(jnp.float32)
    scores = jnp.einsum('qhc,khc->hqk', query, keys) * HEAD_DIM ** (-0.5)
    expo = jnp.exp(scores)
    weights = (expo / lax.optimization_barrier(jnp.sum(expo, axis=-1, keepdims=True))).astype(jnp.bfloat16)
    attended = jnp.einsum('hqk,khc->qhc', weights.astype(jnp.float32), values).astype(jnp.bfloat16)
    attended = attended.reshape(attended.shape[0], -1)
    output = jnp.dot(attended, wo, preferred_element_type=jnp.float32)
    return (gate_row * output).astype(jnp.bfloat16)

def reference(states, start, t_index, coef, mod_table, wqkv, wo):

    def one_step(inputs):
        state, step_index = inputs
        return drift_of(state, step_index, mod_table, wqkv, wo)
    drifts = lax.map(one_step, (states, t_index))
    factors = jnp.take(coef, t_index, axis=0)
    terms = factors[:, None, None] * drifts.astype(jnp.float32)
    return start[None] + jnp.cumsum(terms, axis=0)
```

```python
import jax
import jax.numpy as jnp
from jax import lax
from jax.sharding import Mesh, PartitionSpec as P

HEAD_DIM = 128
TM = ("xl", "y", "core")
SEQ = ("xh", "z")


def send(array, axis, shift):
    size = lax.axis_size(axis)
    return lax.ppermute(array, axis, [(i, (i + shift) % size) for i in range(size)])


def gather_tokens(modded):
    half = modded.shape[0] // 2
    rows = []
    for block in (modded, send(modded, "xh", 1)):
        above = send(block, "z", -1)
        below = send(block, "z", 1)
        far = jnp.concatenate(
            [send(above[:half], "z", -1), send(below[half:], "z", 1)], axis=0
        )
        rows.append([block, above, far, below])
    return rows


def normed(projected):
    per_head = projected.reshape(projected.shape[0], -1, HEAD_DIM)
    scaled = per_head * lax.rsqrt(
        jnp.mean(per_head * per_head, axis=-1, keepdims=True) + 1e-06
    )
    return scaled.astype(jnp.bfloat16)


def on_device(states, start, t_index, coef, mod_table, wqkv, wo):
    state = states[0]
    tokens, width = state.shape
    step = t_index[0]
    modulation = lax.dynamic_index_in_dim(mod_table, step, 0, keepdims=False)
    factor = lax.dynamic_index_in_dim(coef, step, 0, keepdims=False)
    shift_row, scale_row, gate_row = (modulation[0], modulation[1], modulation[2])
    weights_of = [lax.all_gather(wqkv[j], TM, axis=0, tiled=True) for j in range(3)]
    center = jnp.mean(state, axis=-1, keepdims=True)
    spread = jnp.mean((state - center) * (state - center), axis=-1, keepdims=True)
    modded = ((state - center) * lax.rsqrt(spread + 1e-06) * (1.0 + scale_row) + shift_row).astype(
        jnp.bfloat16
    )
    rows = gather_tokens(modded)
    features = jnp.concatenate([block for row in rows for block in row], axis=0)
    projected = [
        jnp.dot(features, w, preferred_element_type=jnp.float32) for w in weights_of
    ]
    query, keys = normed(projected[0]), normed(projected[1])
    values = projected[2].reshape(features.shape[0], -1, HEAD_DIM).astype(jnp.bfloat16)
    scores = jnp.einsum(
        "qhc,khc->hqk", query, keys, preferred_element_type=jnp.float32
    ) * HEAD_DIM ** (-0.5)
    expo = jnp.exp(scores)
    weights = (expo / jnp.sum(expo, axis=-1, keepdims=True)).astype(jnp.bfloat16)
    attended = jnp.einsum(
        "hqk,khc->qhc", weights, values, preferred_element_type=jnp.float32
    ).astype(jnp.bfloat16)
    attended = attended.reshape(attended.shape[0], -1)
    partial = jnp.dot(attended, wo, preferred_element_type=jnp.float32).astype(jnp.bfloat16)
    nx, nz = lax.axis_size("xh"), lax.axis_size("z")
    xh, z = lax.axis_index("xh"), lax.axis_index("z")
    partial = partial.reshape(nx * nz, tokens, width)
    place = [((a + xh) % nx) * nz + (b - z + nz) % nz for a in range(nx) for b in range(nz)]
    partial = jnp.stack([lax.dynamic_index_in_dim(partial, p, 0, keepdims=False) for p in place])
    arrived = lax.all_to_all(partial, SEQ, 0, 0, tiled=False)
    output = jnp.sum(arrived.astype(jnp.float32), axis=0)
    term = ((factor * gate_row) * output).astype(jnp.bfloat16)
    steps = lax.axis_size(TM)
    by_step = lax.all_to_all(term.reshape(steps, tokens // steps, width), TM, 0, 0)
    total = jnp.cumsum(by_step.astype(jnp.float32), axis=0).astype(jnp.bfloat16)
    total = lax.all_to_all(total, TM, 0, 0).reshape(tokens, width)
    return (start + total.astype(jnp.float32))[None]


def solution(mesh):
    wide = Mesh(mesh.devices.reshape(2, 4, 2, 2, 4), TM + SEQ)
    placed = (
        P(TM, SEQ, None),
        P(SEQ, None),
        P(TM),
        P(),
        P(),
        P(None, TM, SEQ),
        P(SEQ, None),
    )
    return jax.shard_map(
        on_device, mesh=wide, in_specs=placed, out_specs=P(TM, SEQ, None), check_vma=False
    )
```

```python
import jax
import jax.numpy as jnp
from jax import lax
from jax.sharding import Mesh, PartitionSpec as P

HEAD_DIM = 128
TM = ("xl", "y", "core")
SEQ = ("xh", "z")


def send(array, axis, shift):
    size = lax.axis_size(axis)
    return lax.ppermute(array, axis, [(i, (i + shift) % size) for i in range(size)])


def after(array, *others):
    return lax.optimization_barrier((array,) + others)[0]


def normed(projected):
    per_head = projected.reshape(projected.shape[0], -1, HEAD_DIM)
    scaled = per_head * lax.rsqrt(
        jnp.mean(per_head * per_head, axis=-1, keepdims=True) + 1e-06
    )
    return scaled.astype(jnp.bfloat16)


def modulated(state, shift_row, scale_row):
    center = jnp.mean(state, axis=-1, keepdims=True)
    spread = jnp.mean((state - center) * (state - center), axis=-1, keepdims=True)
    return ((state - center) * lax.rsqrt(spread + 1e-06) * (1.0 + scale_row) + shift_row).astype(
        jnp.bfloat16
    )


def by_core(modded, rows):
    tokens = modded.shape[0]
    xl, y, core = (lax.axis_index(a) for a in TM)
    nxl, ny, nc = (lax.axis_size(a) for a in TM)
    block = modded.reshape(tokens, nxl, ny, nc, rows)
    first, second = block[:, 0], block[:, 1]
    swap = xl == 1
    near, far = jnp.where(swap, second, first), jnp.where(swap, first, second)
    cols = jnp.stack([near, far], axis=2)
    halves = []
    for c in range(nc):
        one = cols[:, :, :, c].reshape(tokens, -1)
        twice = jnp.concatenate([one, one], axis=1)
        halves.append(
            lax.dynamic_slice_in_dim(twice, y * (nxl * rows), one.shape[1], axis=1)
        )
    mine = jnp.where(core == 0, halves[0], halves[1])
    other = jnp.where(core == 0, halves[1], halves[0])
    return mine, other


def on_device(states, start, t_index, coef, mod_table, wqkv, wo):
    state = states[0]
    tokens, width = state.shape
    rows = wqkv.shape[1]
    half = rows // 2
    step = t_index[0]

    own = wqkv
    a1, b1 = send(own, "y", -1), send(own, "y", 1)
    p = send(own[:2], "xl", 1)

    modulation = lax.dynamic_index_in_dim(mod_table, step, 0, keepdims=False)
    factor = lax.dynamic_index_in_dim(coef, step, 0, keepdims=False)
    shift_row, scale_row, gate_row = (modulation[0], modulation[1], modulation[2])
    modded = modulated(state, shift_row, scale_row)
    mine, other = by_core(modded, rows)
    pair = jnp.stack([mine, send(other, "core", 1)])
    short = tokens // 2

    za, zb = send(pair, "z", -1), send(pair, "z", 1)
    across = send(after(pair, p), "xh", 1)
    zfa = send(za[:, :short], "z", -1)
    zfb = send(zb[:, short:], "z", 1)

    fva = send(after(a1[2, :half], b1), "y", -1)
    fvb = send(after(b1[2, half:], a1), "y", 1)
    gate = after(p, fva, fvb)
    pa, pb = send(gate, "y", -1), send(gate, "y", 1)
    xv = send(after(jnp.stack([own[2], a1[2], b1[2]]), across), "xl", 1)
    farv = jnp.concatenate([fva, fvb], axis=0)

    across = after(across, zfa, zfb)
    xa, xb = send(across, "z", -1), send(across, "z", 1)
    xfa = send(xa[:, :short], "z", -1)
    xfb = send(xb[:, short:], "z", 1)

    fa = send(after(jnp.concatenate([a1[:2, :half], pa[:, :half]], axis=0), pb), "y", -1)
    fb = send(after(jnp.concatenate([b1[:2, half:], pb[:, half:]], axis=0), pa), "y", 1)
    xvf = send(after(farv, xv), "xl", 1)
    far = jnp.concatenate([fa, fb], axis=1)

    features = jnp.concatenate(
        [
            pair, za, zfa, zfb, zb,
            across, xa, xfa, xfb, xb,
        ],
        axis=1,
    )
    count = features.shape[1]
    features = features.reshape(2 * count, -1)
    qk_rows = [
        own[0], p[0], a1[0], pa[0], far[0], far[2], b1[0], pb[0],
    ], [
        own[1], p[1], a1[1], pa[1], far[1], far[3], b1[1], pb[1],
    ]
    v_rows = [own[2], xv[0], a1[2], xv[1], farv, xvf, b1[2], xv[2]]
    projected = []
    for blocks in (qk_rows[0], qk_rows[1], v_rows):
        here = jnp.dot(
            features, jnp.concatenate(blocks, axis=0), preferred_element_type=jnp.float32
        ).reshape(2, count, -1)
        projected.append(
            here[0] + send(here[1].astype(jnp.bfloat16), "core", 1).astype(jnp.float32)
        )
    query, keys = normed(projected[0]), normed(projected[1])
    values = projected[2].reshape(count, -1, HEAD_DIM).astype(jnp.bfloat16)
    scores = jnp.einsum(
        "qhc,khc->hqk", query, keys, preferred_element_type=jnp.float32
    ) * HEAD_DIM ** (-0.5)
    expo = jnp.exp(scores)
    weights = (expo / jnp.sum(expo, axis=-1, keepdims=True)).astype(jnp.bfloat16)
    attended = jnp.einsum(
        "hqk,khc->qhc", weights, values, preferred_element_type=jnp.float32
    ).astype(jnp.bfloat16)
    attended = attended.reshape(attended.shape[0], -1)
    partial = jnp.dot(attended, wo, preferred_element_type=jnp.float32).astype(jnp.bfloat16)
    nx, nz = lax.axis_size("xh"), lax.axis_size("z")
    xh, z = lax.axis_index("xh"), lax.axis_index("z")
    partial = partial.reshape(nx * nz, tokens, width)
    place = [((a + xh) % nx) * nz + (b - z + nz) % nz for a in range(nx) for b in range(nz)]
    partial = jnp.stack([lax.dynamic_index_in_dim(partial, p, 0, keepdims=False) for p in place])
    arrived = lax.all_to_all(partial, SEQ, 0, 0, tiled=False)
    output = jnp.sum(arrived.astype(jnp.float32), axis=0)
    term = ((factor * gate_row) * output).astype(jnp.bfloat16)
    steps = lax.axis_size(TM)
    by_step = lax.all_to_all(term.reshape(steps, tokens // steps, width), TM, 0, 0)
    total = jnp.cumsum(by_step.astype(jnp.float32), axis=0).astype(jnp.bfloat16)
    total = lax.all_to_all(total, TM, 0, 0).reshape(tokens, width)
    return (start + total.astype(jnp.float32))[None]


def solution(mesh):
    wide = Mesh(mesh.devices.reshape(2, 4, 2, 2, 4), TM + SEQ)
    placed = (
        P(TM, SEQ, None),
        P(SEQ, None),
        P(TM),
        P(),
        P(),
        P(None, TM, SEQ),
        P(SEQ, None),
    )
    return jax.shard_map(
        on_device, mesh=wide, in_specs=placed, out_specs=P(TM, SEQ, None), check_vma=False
    )
```

```python
import functools

import jax
import jax.numpy as jnp
from jax import lax
from jax.experimental import pallas as pl
from jax.experimental.pallas import tpu as pltpu
from jax.sharding import Mesh, PartitionSpec as P

HEAD_DIM = 128
TM = ("xl", "y", "core")
SEQ = ("xh", "z")
F32, BF16 = jnp.float32, jnp.bfloat16
VMEM_BYTES = 48 * 1024 * 1024
ROUND = [0, 1, 3, 2]
ORDER = [(0, 2), (1, 2), (1, 1), (1, 3), (0, 1), (0, 3), (1, 0), (0, 0)]


def send(array, axis, shift):
    size = lax.axis_size(axis)
    return lax.ppermute(array, axis, [(i, (i + shift) % size) for i in range(size)])


def after(array, *others):
    return lax.optimization_barrier((array,) + others)[0]


def add(a, b):
    return (a.astype(F32) + b.astype(F32)).astype(BF16)


def modulate_kernel(rows, t_ref, state_ref, mod_ref, coef_ref, mine_ref, other_ref, gate_ref, scratch):
    state = state_ref[0]
    line = pl.ds(lax.rem(t_ref[0], 8), 1)
    shift_row, scale_row = mod_ref[0, line, :], mod_ref[1, line, :]
    gate_ref[...] = mod_ref[2, line, :] * coef_ref[t_ref[0]]
    center = jnp.mean(state, axis=-1, keepdims=True)
    moved = state - center
    spread = jnp.mean(moved * moved, axis=-1, keepdims=True)
    scratch[...] = moved * lax.rsqrt(spread + 1e-06) * (1.0 + scale_row) + shift_row
    xl, y, core = (lax.axis_index(a) for a in TM)
    ny, wide = 4, 2 * rows
    low = core == 0
    for place, dy in enumerate(ROUND):
        mine, other = [], []
        for dxl in range(2):
            chip = lax.rem(xl + dxl, 2) * ny + lax.rem(y + dy, ny)
            block = scratch[:, pl.ds(pl.multiple_of(chip * wide, 128), wide)]
            first, second = block[:, :rows], block[:, rows:]
            mine.append(jnp.where(low, first, second))
            other.append(jnp.where(low, second, first))
        here = slice(place * wide, (place + 1) * wide)
        mine_ref[:, here] = jnp.concatenate(mine, axis=1).astype(BF16)
        other_ref[:, here] = jnp.concatenate(other, axis=1).astype(BF16)


def modulate(states, t_index, mod_table, coef, rows):
    _, tokens, width = states.shape
    half = jax.ShapeDtypeStruct((tokens, width // 2), BF16)
    return pl.pallas_call(
        functools.partial(modulate_kernel, rows),
        out_shape=(half, half, jax.ShapeDtypeStruct((1, width), F32)),
        grid_spec=pltpu.PrefetchScalarGridSpec(
            num_scalar_prefetch=1,
            grid=(1,),
            in_specs=[
                pl.BlockSpec((1, tokens, width), lambda i, t: (0, 0, 0)),
                pl.BlockSpec((3, 8, width), lambda i, t: (0, t[0] // 8, 0)),
                pl.BlockSpec(memory_space=pltpu.SMEM),
            ],
            out_specs=[
                pl.BlockSpec((tokens, width // 2), lambda i, t: (0, 0)),
                pl.BlockSpec((tokens, width // 2), lambda i, t: (0, 0)),
                pl.BlockSpec((1, width), lambda i, t: (0, 0)),
            ],
            scratch_shapes=[pltpu.VMEM((tokens, width), F32)],
        ),
        compiler_params=pltpu.CompilerParams(vmem_limit_bytes=VMEM_BYTES),
        cost_estimate=pl.CostEstimate(flops=1000, bytes_accessed=1000, transcendentals=0),
    )(t_index, states, jnp.transpose(mod_table, (1, 0, 2)), coef)


def attention_kernel(qa, qb, ka, kb, va, vb, out_ref):
    def whole(a, b):
        return a[...] + b[...].astype(F32)

    def normed(x):
        return (x * lax.rsqrt(jnp.mean(x * x, axis=-1, keepdims=True) + 1e-06)).astype(BF16)

    query, keys = normed(whole(qa, qb)), normed(whole(ka, kb))
    values = whole(va, vb).astype(BF16)
    scores = lax.dot_general(
        query, keys, (((1,), (1,)), ((), ())), preferred_element_type=F32
    ) * HEAD_DIM ** (-0.5)
    expo = jnp.exp(scores)
    weights = (expo * (1.0 / jnp.sum(expo, axis=-1, keepdims=True))).astype(BF16)
    out_ref[...] = jnp.dot(weights, values, preferred_element_type=F32).astype(BF16)


def attention(parts):
    count, width = parts[1].shape
    spec = pl.BlockSpec((count, HEAD_DIM), lambda h: (0, h))
    return pl.pallas_call(
        attention_kernel,
        out_shape=jax.ShapeDtypeStruct((count, width), BF16),
        grid=(width // HEAD_DIM,),
        in_specs=[spec] * 6,
        out_specs=spec,
        compiler_params=pltpu.CompilerParams(vmem_limit_bytes=VMEM_BYTES),
        cost_estimate=pl.CostEstimate(
            flops=4 * count * count * width, bytes_accessed=20 * count * width, transcendentals=0
        ),
    )(*parts)


def on_device(states, start, t_index, coef, mod_table, wqkv, wo):
    tokens, width = states.shape[1:]
    rows = wqkv.shape[1]
    half, short = rows // 2, tokens // 2

    own = wqkv
    a1, b1 = send(own, "y", -1), send(own, "y", 1)
    p = send(own[:2], "xl", 1)

    mine, other, gate_row = modulate(states, t_index, mod_table, coef, rows)
    pair = jnp.stack([mine, send(other, "core", 1)])

    za, zb = send(pair, "z", -1), send(pair, "z", 1)
    across = send(after(pair, p), "xh", 1)
    zfa = send(za[:, :short], "z", -1)
    zfb = send(zb[:, short:], "z", 1)

    pa = send(after(jnp.concatenate([p.reshape(2 * rows, -1), a1[2, :half]], axis=0), b1), "y", -1)
    pb = send(after(jnp.concatenate([p.reshape(2 * rows, -1), b1[2, half:]], axis=0), a1), "y", 1)
    farv = jnp.concatenate([pa[2 * rows :], pb[2 * rows :]], axis=0)
    pa, pb = pa[: 2 * rows].reshape(p.shape), pb[: 2 * rows].reshape(p.shape)
    xvo = send(after(own[2], across), "xl", 1)
    xvab = send(after(jnp.stack([a1[2], b1[2]]), xvo), "xl", 1)

    across = after(across, zfa, zfb)
    xa, xb = send(across, "z", -1), send(across, "z", 1)
    xfa = send(after(xa[:, :short], xvo), "z", -1)
    xfb = send(after(xb[:, short:], xvo), "z", 1)

    fa = send(jnp.concatenate([a1[:2, :half], pa[:, :half]], axis=0), "y", -1)
    fb = send(jnp.concatenate([b1[:2, half:], pb[:, half:]], axis=0), "y", 1)
    xvf = send(after(farv, xvab), "xl", 1)
    far = jnp.concatenate([fa, fb], axis=1)

    blocks = {
        (0, 0): pair, (0, 1): za, (0, 2): jnp.concatenate([zfa, zfb], axis=1), (0, 3): zb,
        (1, 0): across, (1, 1): xa, (1, 2): jnp.concatenate([xfa, xfb], axis=1), (1, 3): xb,
    }
    features = jnp.concatenate([blocks[k] for k in ORDER], axis=1)
    count = features.shape[1]
    features = features.reshape(2 * count, -1)
    early = 6 * rows
    parts = []
    begun = [
        jnp.dot(
            features[:, :early],
            jnp.concatenate([own[j], p[j], a1[j], pa[j], b1[j], pb[j]], axis=0),
            preferred_element_type=F32,
        )
        for j in range(2)
    ]
    begun = lax.optimization_barrier(begun)
    for j in range(3):
        if j < 2:
            here = begun[j] + jnp.dot(
                features[:, early:],
                jnp.concatenate([far[j], far[2 + j]], axis=0),
                preferred_element_type=F32,
            )
        else:
            here = jnp.dot(
                features,
                jnp.concatenate([own[2], xvo, a1[2], xvab[0], b1[2], xvab[1], farv, xvf], axis=0),
                preferred_element_type=F32,
            )
        parts += [here, send(here[count:].astype(BF16), "core", 1)]
    attended = attention(parts)

    cut = width // 2
    first = jnp.dot(attended[: 2 * tokens], wo, preferred_element_type=F32).astype(BF16)
    rest = jnp.dot(after(attended[2 * tokens :], first), wo, preferred_element_type=F32)
    part = {k: rest[i * tokens : (i + 1) * tokens] for i, k in enumerate(ORDER[2:])}
    first = first.reshape(2, tokens, width)
    up, down = send(first[:, :, :cut], "z", 1), send(first[:, :, cut:], "z", -1)

    def over_z(dx):
        raised = jnp.concatenate(
            [part[dx, 1][:, :cut] + up[dx].astype(F32), part[dx, 1][:, cut:]], axis=1
        ).astype(BF16)
        lowered = jnp.concatenate(
            [part[dx, 3][:, :cut], part[dx, 3][:, cut:] + down[dx].astype(F32)], axis=1
        ).astype(BF16)
        return (
            part[dx, 0] + send(raised, "z", 1).astype(F32) + send(lowered, "z", -1).astype(F32)
        )

    there = send(over_z(1).astype(BF16), "xh", 1)
    output = over_z(0) + there.astype(F32)
    term = (gate_row * output).astype(BF16)
    steps = lax.axis_size(TM)
    by_step = lax.all_to_all(term.reshape(steps, tokens // steps, width), TM, 0, 0)
    total = jnp.cumsum(by_step.astype(F32), axis=0).astype(BF16)
    total = lax.all_to_all(total, TM, 0, 0).reshape(tokens, width)
    return (start + total.astype(F32))[None]


def solution(mesh):
    wide = Mesh(mesh.devices.reshape(2, 4, 2, 2, 4), TM + SEQ)
    placed = (
        P(TM, SEQ, None),
        P(SEQ, None),
        P(TM),
        P(),
        P(),
        P(None, TM, SEQ),
        P(SEQ, None),
    )
    return jax.shard_map(
        on_device, mesh=wide, in_specs=placed, out_specs=P(TM, SEQ, None), check_vma=False
    )
```

```python
import functools

import jax
import jax.numpy as jnp
from jax import lax
from jax.experimental import pallas as pl
from jax.experimental.pallas import tpu as pltpu
from jax.sharding import Mesh, PartitionSpec as P

HEAD_DIM = 128
TM = ("xl", "y", "core")
SEQ = ("xh", "z")
F32, BF16 = jnp.float32, jnp.bfloat16
VMEM_BYTES = 60 * 1024 * 1024
ROUND = [0, 1, 3, 2]
BLOCKS = [2, 1, 3, 0]


def send(array, axis, shift):
    size = lax.axis_size(axis)
    return lax.ppermute(array, axis, [(i, (i + shift) % size) for i in range(size)])


def after(array, *others):
    return lax.optimization_barrier((array,) + others)[0]


def add(a, b):
    return (a.astype(F32) + b.astype(F32)).astype(BF16)


def modulate_kernel(rows, t_ref, state_ref, mod_ref, coef_ref, mine_ref, other_ref, gate_ref, scratch):
    state = state_ref[0]
    line = pl.ds(lax.rem(t_ref[0], 8), 1)
    shift_row, scale_row = mod_ref[0, line, :], mod_ref[1, line, :]
    gate_ref[...] = mod_ref[2, line, :] * coef_ref[t_ref[0]]
    center = jnp.mean(state, axis=-1, keepdims=True)
    moved = state - center
    spread = jnp.mean(moved * moved, axis=-1, keepdims=True)
    scratch[...] = moved * lax.rsqrt(spread + 1e-06) * (1.0 + scale_row) + shift_row
    xl, y, core = (lax.axis_index(a) for a in TM)
    ny, wide = 4, 2 * rows
    low = core == 0
    for dxl in range(2):
        for pair in range(ny // 2):
            mine, other = [], []
            for dy in ROUND[2 * pair : 2 * pair + 2]:
                chip = lax.rem(xl + dxl, 2) * ny + lax.rem(y + dy, ny)
                block = scratch[:, pl.ds(pl.multiple_of(chip * wide, 128), wide)]
                first, second = block[:, :rows], block[:, rows:]
                mine.append(jnp.where(low, first, second))
                other.append(jnp.where(low, second, first))
            place = dxl * ny // 2 + pair
            here = slice(place * wide, (place + 1) * wide)
            mine_ref[:, here] = jnp.concatenate(mine, axis=1).astype(BF16)
            other_ref[:, here] = jnp.concatenate(other, axis=1).astype(BF16)


def modulate(states, t_index, mod_table, coef, rows):
    _, tokens, width = states.shape
    half = jax.ShapeDtypeStruct((tokens, width // 2), BF16)
    return pl.pallas_call(
        functools.partial(modulate_kernel, rows),
        out_shape=(half, half, jax.ShapeDtypeStruct((1, width), F32)),
        grid_spec=pltpu.PrefetchScalarGridSpec(
            num_scalar_prefetch=1,
            grid=(1,),
            in_specs=[
                pl.BlockSpec((1, tokens, width), lambda i, t: (0, 0, 0)),
                pl.BlockSpec((3, 8, width), lambda i, t: (0, t[0] // 8, 0)),
                pl.BlockSpec(memory_space=pltpu.SMEM),
            ],
            out_specs=[
                pl.BlockSpec((tokens, width // 2), lambda i, t: (0, 0)),
                pl.BlockSpec((tokens, width // 2), lambda i, t: (0, 0)),
                pl.BlockSpec((1, width), lambda i, t: (0, 0)),
            ],
            scratch_shapes=[pltpu.VMEM((tokens, width), F32)],
        ),
        compiler_params=pltpu.CompilerParams(vmem_limit_bytes=VMEM_BYTES),
        cost_estimate=pl.CostEstimate(flops=1000, bytes_accessed=1000, transcendentals=0),
    )(t_index, states, jnp.transpose(mod_table, (1, 0, 2)), coef)


def normed(x):
    return (x * lax.rsqrt(jnp.mean(x * x, axis=-1, keepdims=True) + 1e-06)).astype(BF16)


def attend(query, keys, values):
    scores = lax.dot_general(query, keys, (((1,), (1,)), ((), ())), preferred_element_type=F32)
    expo = jnp.exp(scores * HEAD_DIM ** (-0.5))
    total = jnp.sum(expo, axis=-1, keepdims=True)
    return (
        jnp.dot(expo.astype(BF16), values, preferred_element_type=F32) * (1.0 / total)
    ).astype(BF16)


def first_kernel(head, q0, q1, qb, k0, k1, kb, v0, v1, vb, query_ref, keys_ref, values_ref, out_ref):
    half = q0.shape[0]
    for dx, (q, k, v) in enumerate(((q0, k0, v0), (q1, k1, v1))):
        rows = slice(dx * half, (dx + 1) * half)
        query_ref[rows] = normed(q[...] + qb[rows].astype(F32))
        keys_ref[rows] = normed(k[...] + kb[rows].astype(F32))
        values_ref[rows] = (v[...] + vb[rows].astype(F32)).astype(BF16)
    out_ref[...] = attend(query_ref[half : half + head], keys_ref[...], values_ref[...])


def second_kernel(head, query_ref, keys_ref, values_ref, out_ref):
    half = query_ref.shape[0] // 2
    query = jnp.concatenate([query_ref[:half], query_ref[half + head :]], axis=0)
    out_ref[...] = attend(query, keys_ref[...], values_ref[...])


def attention_call(kernel, operands, heights, shapes):
    count, width = operands[-1].shape

    def spec(rows):
        return pl.BlockSpec((rows, HEAD_DIM), lambda h: (0, h))

    return pl.pallas_call(
        kernel,
        out_shape=[jax.ShapeDtypeStruct((rows, width), BF16) for rows in shapes],
        grid=(width // HEAD_DIM,),
        in_specs=[spec(rows) for rows in heights],
        out_specs=[spec(rows) for rows in shapes],
        compiler_params=pltpu.CompilerParams(vmem_limit_bytes=16 * 1024 * 1024),
        cost_estimate=pl.CostEstimate(
            flops=4 * shapes[-1] * count * width, bytes_accessed=8 * count * width, transcendentals=0
        ),
    )(*operands)


def on_device(states, start, t_index, coef, mod_table, wqkv, wo):
    tokens, width = states.shape[1:]
    rows = wqkv.shape[1]
    half, short = rows // 2, tokens // 2

    own = wqkv
    a1, b1 = send(own, "y", -1), send(own, "y", 1)
    p = send(own[:2], "xl", 1)

    mine, other, gate_row = modulate(states, t_index, mod_table, coef, rows)
    pair = jnp.stack([mine, send(other, "core", 1)])

    za, zb = send(pair, "z", -1), send(pair, "z", 1)
    across = send(after(pair, p), "xh", 1)
    zfa = send(after(za[:, :short], zb), "z", -1)
    zfb = send(after(zb[:, short:], za), "z", 1)

    xv = send(after(jnp.stack([own[2], a1[2], b1[2]]), across), "xl", 1)
    fa = send(after(a1[:, :half], b1), "y", -1)
    fb = send(after(b1[:, half:], a1), "y", 1)
    far = jnp.concatenate([fa, fb], axis=1)

    distant = after(across, zfa, zfb)
    xa, xb = send(distant, "z", -1), send(distant, "z", 1)
    xfa = send(after(xa[:, :short], xb), "z", -1)
    xfb = send(after(xb[:, short:], xa), "z", 1)

    near = after(p, fa, fb)
    pa, pb = send(near, "y", -1), send(near, "y", 1)
    xvf = send(after(far[2], xv), "xl", 1)
    pfa = send(after(pa[:, :half], pb), "y", -1)
    pfb = send(after(pb[:, half:], pa), "y", 1)
    pfar = jnp.concatenate([pfa, pfb], axis=1)

    features = []
    for near, above, below, ends in ((pair, za, zb, (zfa, zfb)), (across, xa, xb, (xfa, xfb))):
        rowed = jnp.concatenate([*ends, above, below, near], axis=1)
        features.append(rowed.reshape(2 * rowed.shape[1], -1))
    count = features[0].shape[0]

    def product(begin, weights):
        stop = begin + weights[0].shape[0]
        return [
            [jnp.dot(f[:, begin:stop], w, preferred_element_type=F32) for w in weights]
            for f in features
        ]

    def plus(sofar, more):
        return [[a + b for a, b in zip(x, y)] for x, y in zip(sofar, more)]

    stacked = [
        [jnp.concatenate(blocks, axis=0) for blocks in stage]
        for stage in (
            [[own[j], a1[j], b1[j], far[j]] for j in range(3)],
            [[p[0], pa[0]], [p[1], pa[1]], [xv[0], xv[1]]],
            [[pb[0], pfar[0]], [pb[1], pfar[1]], [xv[2], xvf]],
        )
    ]
    features[1] = after(features[1], pa, pb)
    stacked[1] = [after(w, xv) for w in stacked[1]]
    begun = [lax.optimization_barrier(x) for x in product(0, stacked[0])]
    begun = [lax.optimization_barrier(x) for x in plus(begun, product(4 * rows, stacked[1]))]
    begun = plus(begun, product(6 * rows, stacked[2]))
    parts = []
    for j in range(3):
        mates = jnp.concatenate([x[j][count // 2 :] for x in begun], axis=0).astype(BF16)
        parts += [begun[0][j], begun[1][j], send(mates, "core", 1)]

    cut, half, head = width // 2, count // 2, 3 * tokens
    query, keys, values, attended = attention_call(
        functools.partial(first_kernel, head), parts, (half, half, count) * 3,
        (count, count, count, head),
    )
    first = jnp.dot(attended, wo, preferred_element_type=F32).astype(BF16)
    far1, above1, below1 = (first[i * tokens : (i + 1) * tokens] for i in range(3))
    joins = [send(far1[:, :cut], "xh", 1), send(far1[:, cut:], "xh", 1)]
    up1, down1 = send(above1, "z", 1), send(below1, "z", -1)
    (attended,) = attention_call(
        functools.partial(second_kernel, head), (after(query, joins[0]), keys, values),
        (count,) * 3, (count - head,),
    )
    rest = jnp.dot(attended, wo, preferred_element_type=F32)
    far0, above0, below0, near0, near1 = (rest[i * tokens : (i + 1) * tokens] for i in range(5))
    free = send(above0[:, cut:].astype(BF16), "z", 1), send(below0[:, :cut].astype(BF16), "z", -1)
    up = send((far0[:, :cut] + joins[0].astype(F32)).astype(BF16), "z", 1)
    down = send((far0[:, cut:] + joins[1].astype(F32)).astype(BF16), "z", -1)
    there = send((near1 + up1.astype(F32) + down1.astype(F32)).astype(BF16), "xh", 1)
    bound = (
        send((above0[:, :cut] + up.astype(F32)).astype(BF16), "z", 1),
        send((below0[:, cut:] + down.astype(F32)).astype(BF16), "z", -1),
    )
    output = (
        near0
        + jnp.concatenate([bound[0], free[0]], axis=1).astype(F32)
        + jnp.concatenate([free[1], bound[1]], axis=1).astype(F32)
        + there.astype(F32)
    )
    term = (gate_row * output).astype(BF16)
    steps = lax.axis_size(TM)
    by_step = lax.all_to_all(term.reshape(steps, tokens // steps, width), TM, 0, 0)
    total = jnp.cumsum(by_step.astype(F32), axis=0).astype(BF16)
    total = lax.all_to_all(total, TM, 0, 0).reshape(tokens, width)
    return (start + total.astype(F32))[None]


def solution(mesh):
    wide = Mesh(mesh.devices.reshape(2, 4, 2, 2, 4), TM + SEQ)
    placed = (
        P(TM, SEQ, None),
        P(SEQ, None),
        P(TM),
        P(),
        P(),
        P(None, TM, SEQ),
        P(SEQ, None),
    )
    return jax.shard_map(
        on_device, mesh=wide, in_specs=placed, out_specs=P(TM, SEQ, None), check_vma=False
    )
```

```python
import functools

import jax
import jax.numpy as jnp
from jax import lax
from jax.experimental import pallas as pl
from jax.experimental.pallas import tpu as pltpu
from jax.sharding import Mesh, PartitionSpec as P

HEAD_DIM = 128
TM = ("xl", "y", "core")
SEQ = ("xh", "z")
F32, BF16 = jnp.float32, jnp.bfloat16
VMEM_BYTES = 60 * 1024 * 1024
COLUMNS = [(0, 0), (1, 0), (0, 1), (1, 1), (3, 0), (3, 1), (2, 0), (2, 1)]
BLOCKS = [2, 1, 3, 0]


def send(array, axis, shift):
    size = lax.axis_size(axis)
    return lax.ppermute(array, axis, [(i, (i + shift) % size) for i in range(size)])


def after(array, *others):
    return lax.optimization_barrier((array,) + others)[0]


def add(a, b):
    return (a.astype(F32) + b.astype(F32)).astype(BF16)


def modulate_kernel(rows, t_ref, state_ref, mod_ref, coef_ref, mine_ref, other_ref, gate_ref, scratch):
    state = state_ref[0]
    line = pl.ds(lax.rem(t_ref[0], 8), 1)
    shift_row, scale_row = mod_ref[0, line, :], mod_ref[1, line, :]
    gate_ref[...] = mod_ref[2, line, :] * coef_ref[t_ref[0]]
    center = jnp.mean(state, axis=-1, keepdims=True)
    moved = state - center
    spread = jnp.mean(moved * moved, axis=-1, keepdims=True)
    scratch[...] = moved * lax.rsqrt(spread + 1e-06) * (1.0 + scale_row) + shift_row
    xl, y, core = (lax.axis_index(a) for a in TM)
    ny, wide = 4, 2 * rows
    low = core == 0
    for place in range(0, len(COLUMNS), 2):
        mine, other = [], []
        for dy, dxl in COLUMNS[place : place + 2]:
            chip = lax.rem(xl + dxl, 2) * ny + lax.rem(y + dy, ny)
            block = scratch[:, pl.ds(pl.multiple_of(chip * wide, 128), wide)]
            first, second = block[:, :rows], block[:, rows:]
            mine.append(jnp.where(low, first, second))
            other.append(jnp.where(low, second, first))
        here = slice(place * rows, (place + 2) * rows)
        mine_ref[:, here] = jnp.concatenate(mine, axis=1).astype(BF16)
        other_ref[:, here] = jnp.concatenate(other, axis=1).astype(BF16)


def modulate(states, t_index, mod_table, coef, rows):
    _, tokens, width = states.shape
    half = jax.ShapeDtypeStruct((tokens, width // 2), BF16)
    return pl.pallas_call(
        functools.partial(modulate_kernel, rows),
        out_shape=(half, half, jax.ShapeDtypeStruct((1, width), F32)),
        grid_spec=pltpu.PrefetchScalarGridSpec(
            num_scalar_prefetch=1,
            grid=(1,),
            in_specs=[
                pl.BlockSpec((1, tokens, width), lambda i, t: (0, 0, 0)),
                pl.BlockSpec((3, 8, width), lambda i, t: (0, t[0] // 8, 0)),
                pl.BlockSpec(memory_space=pltpu.SMEM),
            ],
            out_specs=[
                pl.BlockSpec((tokens, width // 2), lambda i, t: (0, 0)),
                pl.BlockSpec((tokens, width // 2), lambda i, t: (0, 0)),
                pl.BlockSpec((1, width), lambda i, t: (0, 0)),
            ],
            scratch_shapes=[pltpu.VMEM((tokens, width), F32)],
        ),
        compiler_params=pltpu.CompilerParams(vmem_limit_bytes=VMEM_BYTES),
        cost_estimate=pl.CostEstimate(flops=1000, bytes_accessed=1000, transcendentals=0),
    )(t_index, states, jnp.transpose(mod_table, (1, 0, 2)), coef)


def normed(x):
    return (x * lax.rsqrt(jnp.mean(x * x, axis=-1, keepdims=True) + 1e-06)).astype(BF16)


def attend(query, keys, values):
    scores = lax.dot_general(query, keys, (((1,), (1,)), ((), ())), preferred_element_type=F32)
    expo = jnp.exp(scores * HEAD_DIM ** (-0.5))
    total = jnp.sum(expo, axis=-1, keepdims=True)
    return (
        jnp.dot(expo.astype(BF16), values, preferred_element_type=F32) * (1.0 / total)
    ).astype(BF16)


def first_kernel(head, q0, q1, qb, k0, k1, kb, v0, v1, vb, query_ref, keys_ref, values_ref, out_ref):
    half = q0.shape[0]
    for dx, (q, k, v) in enumerate(((q0, k0, v0), (q1, k1, v1))):
        rows = slice(dx * half, (dx + 1) * half)
        query_ref[rows] = normed(q[...] + qb[rows].astype(F32))
        keys_ref[rows] = normed(k[...] + kb[rows].astype(F32))
        values_ref[rows] = (v[...] + vb[rows].astype(F32)).astype(BF16)
    out_ref[...] = attend(query_ref[half : half + head], keys_ref[...], values_ref[...])


def second_kernel(head, query_ref, keys_ref, values_ref, out_ref):
    half = query_ref.shape[0] // 2
    query = jnp.concatenate([query_ref[:half], query_ref[half + head :]], axis=0)
    out_ref[...] = attend(query, keys_ref[...], values_ref[...])


def attention_call(kernel, operands, heights, shapes):
    count, width = operands[-1].shape

    def spec(rows):
        return pl.BlockSpec((rows, HEAD_DIM), lambda h: (0, h))

    return pl.pallas_call(
        kernel,
        out_shape=[jax.ShapeDtypeStruct((rows, width), BF16) for rows in shapes],
        grid=(width // HEAD_DIM,),
        in_specs=[spec(rows) for rows in heights],
        out_specs=[spec(rows) for rows in shapes],
        compiler_params=pltpu.CompilerParams(vmem_limit_bytes=16 * 1024 * 1024),
        cost_estimate=pl.CostEstimate(
            flops=4 * shapes[-1] * count * width, bytes_accessed=8 * count * width, transcendentals=0
        ),
    )(*operands)


def on_device(states, start, t_index, coef, mod_table, wqkv, wo):
    tokens, width = states.shape[1:]
    rows = wqkv.shape[1]
    half, short = rows // 2, tokens // 2

    own = wqkv
    a1, b1 = send(own, "y", -1), send(own, "y", 1)
    p = send(own[:2], "xl", 1)

    mine, other, gate_row = modulate(states, t_index, mod_table, coef, rows)
    pair = jnp.stack([mine, send(other, "core", 1)])

    za, zb = send(pair, "z", -1), send(pair, "z", 1)
    across = send(after(pair, p), "xh", 1)
    near = after(p, za, zb)
    pa, pb = send(near, "y", -1), send(near, "y", 1)
    zfa = send(after(za[:, :short], a1, b1), "z", -1)
    zfb = send(after(zb[:, short:], a1, b1), "z", 1)

    xv = send(after(jnp.stack([own[2], a1[2], b1[2]]), across), "xl", 1)
    distant = after(across, zfa, zfb)
    xa, xb = send(distant, "z", -1), send(distant, "z", 1)

    fa = send(jnp.concatenate([a1[:, :half], pa[:, :half]], axis=0), "y", -1)
    fb = send(jnp.concatenate([b1[:, half:], pb[:, half:]], axis=0), "y", 1)
    xfa = send(after(xa[:, :short], xb), "z", -1)
    xfb = send(after(xb[:, short:], xa), "z", 1)
    vfa = send(after(xv[1, :half], xfa, xfb), "y", -1)
    vfb = send(after(xv[2, half:], xfa, xfb), "y", 1)
    far = jnp.concatenate([fa, fb], axis=1)
    vfar = jnp.concatenate([vfa, vfb], axis=0)

    features = []
    for near, above, below, ends in ((pair, za, zb, (zfa, zfb)), (across, xa, xb, (xfa, xfb))):
        rowed = jnp.concatenate([*ends, above, below, near], axis=1)
        features.append(rowed.reshape(2 * rowed.shape[1], -1))
    count = features[0].shape[0]

    def product(begin, blocks):
        stop = begin + len(blocks) * rows
        weight = jnp.concatenate(blocks, axis=0)
        return [jnp.dot(f[:, begin:stop], weight, preferred_element_type=F32) for f in features]

    def plus(sofar, more):
        return [a + b for a, b in zip(sofar, more)]

    held = lax.optimization_barrier
    begun = [[held(x) for x in product(0, [own[j], a1[j], p[j], pa[j], b1[j], pb[j]])] for j in range(2)]
    begun.append([held(x) for x in product(0, [own[2], a1[2]])])
    begun[2] = [held(x) for x in plus(begun[2], product(2 * rows, [xv[0], xv[1], b1[2], xv[2]]))]
    last = [[far[0], far[3]], [far[1], far[4]], [far[2], vfar]]
    begun = [plus(x, product(6 * rows, blocks)) for x, blocks in zip(begun, last)]
    parts = []
    for j in range(3):
        mates = jnp.concatenate([x[count // 2 :] for x in begun[j]], axis=0).astype(BF16)
        parts += [*begun[j], send(mates, "core", 1)]

    cut, half, head = width // 2, count // 2, 3 * tokens
    query, keys, values, attended = attention_call(
        functools.partial(first_kernel, head), parts, (half, half, count) * 3,
        (count, count, count, head),
    )
    first = jnp.dot(attended, wo, preferred_element_type=F32).astype(BF16)
    far1, above1, below1 = (first[i * tokens : (i + 1) * tokens] for i in range(3))
    up1, down1 = send(above1, "z", 1), send(below1, "z", -1)
    quarter = cut // 2
    joins = [send(far1[:, :quarter], "xh", 1), send(far1[:, quarter:], "xh", 1)]
    (attended,) = attention_call(
        functools.partial(second_kernel, head), (after(query, joins[0]), keys, values),
        (count,) * 3, (count - head,),
    )
    rest = jnp.dot(attended, wo, preferred_element_type=F32)
    far0, above0, below0, near0, near1 = (rest[i * tokens : (i + 1) * tokens] for i in range(5))
    far0 = (far0 + jnp.concatenate(joins, axis=1).astype(F32)).astype(BF16)
    up, down = send(far0[:, :cut], "z", 1), send(far0[:, cut:], "z", -1)
    free = (
        send(after(above0[:, cut:].astype(BF16), up1, down1), "z", 1),
        send(after(below0[:, :cut].astype(BF16), up1, down1), "z", -1),
    )
    near1 = after(near1, far0)
    there = send((near1 + up1.astype(F32) + down1.astype(F32)).astype(BF16), "xh", 1)
    bound = (
        send((above0[:, :cut] + up.astype(F32)).astype(BF16), "z", 1),
        send((below0[:, cut:] + down.astype(F32)).astype(BF16), "z", -1),
    )
    output = (
        near0
        + jnp.concatenate([bound[0], free[0]], axis=1).astype(F32)
        + jnp.concatenate([free[1], bound[1]], axis=1).astype(F32)
        + there.astype(F32)
    )
    term = (gate_row * output).astype(BF16)
    steps = lax.axis_size(TM)
    by_step = lax.all_to_all(term.reshape(steps, tokens // steps, width), TM, 0, 0)
    total = jnp.cumsum(by_step.astype(F32), axis=0).astype(BF16)
    total = lax.all_to_all(total, TM, 0, 0).reshape(tokens, width)
    return (start + total.astype(F32))[None]


def solution(mesh):
    wide = Mesh(mesh.devices.reshape(2, 4, 2, 2, 4), TM + SEQ)
    placed = (
        P(TM, SEQ, None),
        P(SEQ, None),
        P(TM),
        P(),
        P(),
        P(None, TM, SEQ),
        P(SEQ, None),
    )
    return jax.shard_map(
        on_device, mesh=wide, in_specs=placed, out_specs=P(TM, SEQ, None), check_vma=False
    )
```

```python
import functools

import jax
import jax.numpy as jnp
from jax import lax
from jax.experimental import pallas as pl
from jax.experimental.pallas import tpu as pltpu
from jax.sharding import Mesh, PartitionSpec as P

HEAD_DIM = 128
TM = ("xl", "y", "core")
SEQ = ("xh", "z")
F32, BF16 = jnp.float32, jnp.bfloat16
VMEM_BYTES = 60 * 1024 * 1024
COLUMNS = [(0, 0), (1, 0), (0, 1), (1, 1), (3, 0), (3, 1), (2, 0), (2, 1)]
BLOCKS = [2, 1, 3, 0]


def send(array, axis, shift):
    size = lax.axis_size(axis)
    return lax.ppermute(array, axis, [(i, (i + shift) % size) for i in range(size)])


def after(array, *others):
    return lax.optimization_barrier((array,) + others)[0]


def add(a, b):
    return (a.astype(F32) + b.astype(F32)).astype(BF16)


def modulate_kernel(rows, t_ref, state_ref, mod_ref, coef_ref, mine_ref, other_ref, gate_ref, scratch):
    state = state_ref[0]
    line = pl.ds(lax.rem(t_ref[0], 8), 1)
    shift_row, scale_row = mod_ref[0, line, :], mod_ref[1, line, :]
    gate_ref[...] = mod_ref[2, line, :] * coef_ref[t_ref[0]]
    center = jnp.mean(state, axis=-1, keepdims=True)
    moved = state - center
    spread = jnp.mean(moved * moved, axis=-1, keepdims=True)
    scratch[...] = moved * lax.rsqrt(spread + 1e-06) * (1.0 + scale_row) + shift_row
    xl, y, core = (lax.axis_index(a) for a in TM)
    ny, wide = 4, 2 * rows
    low = core == 0
    for place in range(0, len(COLUMNS), 2):
        mine, other = [], []
        for dy, dxl in COLUMNS[place : place + 2]:
            chip = lax.rem(xl + dxl, 2) * ny + lax.rem(y + dy, ny)
            block = scratch[:, pl.ds(pl.multiple_of(chip * wide, 128), wide)]
            first, second = block[:, :rows], block[:, rows:]
            mine.append(jnp.where(low, first, second))
            other.append(jnp.where(low, second, first))
        here = slice(place * rows, (place + 2) * rows)
        mine_ref[:, here] = jnp.concatenate(mine, axis=1).astype(BF16)
        other_ref[:, here] = jnp.concatenate(other, axis=1).astype(BF16)


def modulate(states, t_index, mod_table, coef, rows):
    _, tokens, width = states.shape
    half = jax.ShapeDtypeStruct((tokens, width // 2), BF16)
    return pl.pallas_call(
        functools.partial(modulate_kernel, rows),
        out_shape=(half, half, jax.ShapeDtypeStruct((1, width), F32)),
        grid_spec=pltpu.PrefetchScalarGridSpec(
            num_scalar_prefetch=1,
            grid=(1,),
            in_specs=[
                pl.BlockSpec((1, tokens, width), lambda i, t: (0, 0, 0)),
                pl.BlockSpec((3, 8, width), lambda i, t: (0, t[0] // 8, 0)),
                pl.BlockSpec(memory_space=pltpu.SMEM),
            ],
            out_specs=[
                pl.BlockSpec((tokens, width // 2), lambda i, t: (0, 0)),
                pl.BlockSpec((tokens, width // 2), lambda i, t: (0, 0)),
                pl.BlockSpec((1, width), lambda i, t: (0, 0)),
            ],
            scratch_shapes=[pltpu.VMEM((tokens, width), F32)],
        ),
        compiler_params=pltpu.CompilerParams(vmem_limit_bytes=VMEM_BYTES),
        cost_estimate=pl.CostEstimate(flops=1000, bytes_accessed=1000, transcendentals=0),
    )(t_index, states, jnp.transpose(mod_table, (1, 0, 2)), coef)


def normed(x):
    return (x * lax.rsqrt(jnp.mean(x * x, axis=-1, keepdims=True) + 1e-06)).astype(BF16)


def attend(query, keys, values):
    scores = lax.dot_general(query, keys, (((1,), (1,)), ((), ())), preferred_element_type=F32)
    expo = jnp.exp(scores * HEAD_DIM ** (-0.5))
    total = jnp.sum(expo, axis=-1, keepdims=True)
    return (
        jnp.dot(expo.astype(BF16), values, preferred_element_type=F32) * (1.0 / total)
    ).astype(BF16)


def first_kernel(head, q, qb, k, kb, v, vb, query_ref, keys_ref, values_ref, out_ref):
    half = v.shape[0] // 2
    for h in range(v.shape[1] // HEAD_DIM):
        at = slice(h * HEAD_DIM, (h + 1) * HEAD_DIM)
        query = normed(q[:, at] + qb[:, at].astype(F32))
        keys = normed(k[:, at] + kb[:, at].astype(F32))
        values = (v[:, at] + vb[:, at].astype(F32)).astype(BF16)
        query_ref[:, at], keys_ref[:, at], values_ref[:, at] = query, keys, values
        out_ref[:, at] = attend(query[half : half + head], keys, values)


def second_kernel(head, query_ref, keys_ref, values_ref, out_ref):
    half = query_ref.shape[0] // 2
    for h in range(query_ref.shape[1] // HEAD_DIM):
        at = slice(h * HEAD_DIM, (h + 1) * HEAD_DIM)
        query = jnp.concatenate([query_ref[:half, at], query_ref[half + head :, at]], axis=0)
        out_ref[:, at] = attend(query, keys_ref[:, at], values_ref[:, at])


def last_kernel(matrices, f0, f1, far, extra, *refs):
    rows, count = far.shape[1], f0.shape[0]
    half, each = count // 2, len(matrices)
    for i, j in enumerate(matrices):
        mate = far[3 + j] if j < 2 else extra[...]
        weight = jnp.concatenate([far[j], mate], axis=0)
        own_ref, mate_ref = refs[2 * each + 2 * i : 2 * each + 2 * i + 2]
        for dx, f in enumerate((f0, f1)):
            total = refs[2 * i + dx][...] + jnp.dot(
                f[:, 6 * rows :], weight, preferred_element_type=F32
            )
            own_ref[dx * half : (dx + 1) * half] = total[:half]
            mate_ref[dx * half : (dx + 1) * half] = total[half:].astype(BF16)


def local_call(kernel, operands, shapes, flops):
    whole = pl.BlockSpec(memory_space=pltpu.VMEM)
    return pl.pallas_call(
        kernel,
        out_shape=[jax.ShapeDtypeStruct(*shape) for shape in shapes],
        in_specs=[whole] * len(operands),
        out_specs=[whole] * len(shapes),
        compiler_params=pltpu.CompilerParams(vmem_limit_bytes=24 * 1024 * 1024),
        cost_estimate=pl.CostEstimate(flops=flops, bytes_accessed=1000, transcendentals=0),
    )(*operands)


def on_device(states, start, t_index, coef, mod_table, wqkv, wo):
    tokens, width = states.shape[1:]
    rows = wqkv.shape[1]
    half, short = rows // 2, tokens // 2

    own = wqkv
    a1, b1 = send(own, "y", -1), send(own, "y", 1)
    p = send(own[:2], "xl", 1)

    mine, other, gate_row = modulate(states, t_index, mod_table, coef, rows)
    pair = jnp.stack([mine, send(other, "core", 1)])

    za, zb = send(pair, "z", -1), send(pair, "z", 1)
    across = send(after(pair, p), "xh", 1)
    near = after(p, za, zb)
    pa, pb = send(near, "y", -1), send(near, "y", 1)
    zfa = send(after(za[:, :short], a1, b1), "z", -1)
    zfb = send(after(zb[:, short:], a1, b1), "z", 1)

    xv = send(after(jnp.stack([own[2], a1[2], b1[2]]), across), "xl", 1)
    distant = after(across, zfa, zfb)
    xa, xb = send(distant, "z", -1), send(distant, "z", 1)

    fa = send(jnp.concatenate([a1[:, :half], pa[:, :half]], axis=0), "y", -1)
    fb = send(jnp.concatenate([b1[:, half:], pb[:, half:]], axis=0), "y", 1)
    xfa = send(after(xa[:, :short], xb), "z", -1)
    xfb = send(after(xb[:, short:], xa), "z", 1)
    vfa = send(after(xv[1, :half], xfa, xfb), "y", -1)
    vfb = send(after(xv[2, half:], xfa, xfb), "y", 1)
    far = jnp.concatenate([fa, fb], axis=1)
    vfar = jnp.concatenate([vfa, vfb], axis=0)

    features = []
    for near, above, below, ends in ((pair, za, zb, (zfa, zfb)), (across, xa, xb, (xfa, xfb))):
        rowed = jnp.concatenate([*ends, above, below, near], axis=1)
        features.append(rowed.reshape(2 * rowed.shape[1], -1))
    count = features[0].shape[0]

    def product(begin, blocks):
        stop = begin + len(blocks) * rows
        weight = jnp.concatenate(blocks, axis=0)
        return [jnp.dot(f[:, begin:stop], weight, preferred_element_type=F32) for f in features]

    def plus(sofar, more):
        return [a + b for a, b in zip(sofar, more)]

    held = lax.optimization_barrier
    begun = [[held(x) for x in product(0, [own[j], a1[j], p[j], pa[j], b1[j], pb[j]])] for j in range(2)]
    begun.append([held(x) for x in product(0, [own[2], a1[2]])])
    begun[2] = [held(x) for x in plus(begun[2], product(2 * rows, [xv[0], xv[1], b1[2], xv[2]]))]
    columns = wqkv.shape[2]
    one = (count, columns)
    q, q_mates, k, k_mates = local_call(
        functools.partial(last_kernel, (0, 1)), (*features, far, far, *begun[0], *begun[1]),
        [(one, F32), (one, BF16)] * 2, 1000,
    )
    v, v_mates = local_call(
        functools.partial(last_kernel, (2,)), (*features, far, vfar, *begun[2]),
        [(one, F32), (one, BF16)], 8 * count * rows * columns,
    )
    parts = (q, send(q_mates, "core", 1), k, send(k_mates, "core", 1), v, send(v_mates, "core", 1))

    cut, head = width // 2, 3 * tokens
    query, keys, values, attended = local_call(
        functools.partial(first_kernel, head), parts, [(one, BF16)] * 3 + [((head, columns), BF16)],
        4 * head * count * columns,
    )
    first = jnp.dot(attended, wo, preferred_element_type=F32).astype(BF16)
    far1, above1, below1 = (first[i * tokens : (i + 1) * tokens] for i in range(3))
    up1, down1 = send(above1, "z", 1), send(below1, "z", -1)
    quarter = cut // 2
    joins = [send(far1[:, :quarter], "xh", 1), send(far1[:, quarter:], "xh", 1)]
    (attended,) = local_call(
        functools.partial(second_kernel, head), (after(query, joins[0]), keys, values),
        [((count - head, columns), BF16)], 4 * (count - head) * count * columns,
    )
    rest = jnp.dot(attended, wo, preferred_element_type=F32)
    far0, above0, below0, near0, near1 = (rest[i * tokens : (i + 1) * tokens] for i in range(5))
    far0 = (far0 + jnp.concatenate(joins, axis=1).astype(F32)).astype(BF16)
    up, down = send(far0[:, :cut], "z", 1), send(far0[:, cut:], "z", -1)
    free = (
        send(after(above0[:, cut:].astype(BF16), up1, down1), "z", 1),
        send(after(below0[:, :cut].astype(BF16), up1, down1), "z", -1),
    )
    near1 = after(near1, far0)
    there = send((near1 + up1.astype(F32) + down1.astype(F32)).astype(BF16), "xh", 1)
    bound = (
        send((above0[:, :cut] + up.astype(F32)).astype(BF16), "z", 1),
        send((below0[:, cut:] + down.astype(F32)).astype(BF16), "z", -1),
    )
    output = (
        near0
        + jnp.concatenate([bound[0], free[0]], axis=1).astype(F32)
        + jnp.concatenate([free[1], bound[1]], axis=1).astype(F32)
        + there.astype(F32)
    )
    term = (gate_row * output).astype(BF16)
    steps = lax.axis_size(TM)
    by_step = lax.all_to_all(term.reshape(steps, tokens // steps, width), TM, 0, 0)
    total = jnp.cumsum(by_step.astype(F32), axis=0).astype(BF16)
    total = lax.all_to_all(total, TM, 0, 0).reshape(tokens, width)
    return (start + total.astype(F32))[None]


def solution(mesh):
    wide = Mesh(mesh.devices.reshape(2, 4, 2, 2, 4), TM + SEQ)
    placed = (
        P(TM, SEQ, None),
        P(SEQ, None),
        P(TM),
        P(),
        P(),
        P(None, TM, SEQ),
        P(SEQ, None),
    )
    return jax.shard_map(
        on_device, mesh=wide, in_specs=placed, out_specs=P(TM, SEQ, None), check_vma=False
    )
```

```python
import functools

import jax
import jax.numpy as jnp
from jax import lax
from jax.experimental import pallas as pl
from jax.experimental.pallas import tpu as pltpu
from jax.sharding import Mesh, PartitionSpec as P

HEAD_DIM = 128
TM = ("xl", "y", "core")
SEQ = ("xh", "z")
F32, BF16 = jnp.float32, jnp.bfloat16
VMEM_BYTES = 60 * 1024 * 1024
COLUMNS = [(0, 0), (1, 0), (0, 1), (1, 1), (3, 0), (3, 1), (2, 0), (2, 1)]
BLOCKS = [2, 1, 3, 0]


def send(array, axis, shift):
    size = lax.axis_size(axis)
    return lax.ppermute(array, axis, [(i, (i + shift) % size) for i in range(size)])


def after(array, *others):
    return lax.optimization_barrier((array,) + others)[0]


def add(a, b):
    return (a.astype(F32) + b.astype(F32)).astype(BF16)


def modulate_kernel(rows, t_ref, state_ref, mod_ref, coef_ref, mine_ref, other_ref, gate_ref, scratch):
    state = state_ref[0]
    line = pl.ds(lax.rem(t_ref[0], 8), 1)
    shift_row, scale_row = mod_ref[0, line, :], mod_ref[1, line, :]
    gate_ref[...] = mod_ref[2, line, :] * coef_ref[t_ref[0]]
    center = jnp.mean(state, axis=-1, keepdims=True)
    moved = state - center
    spread = jnp.mean(moved * moved, axis=-1, keepdims=True)
    scratch[...] = (moved * lax.rsqrt(spread + 1e-06) * (1.0 + scale_row) + shift_row).astype(BF16)
    xl, y, core = (lax.axis_index(a) for a in TM)
    ny, wide = 4, 2 * rows
    low = core == 0
    for place in range(0, len(COLUMNS), 2):
        mine, other = [], []
        for dy, dxl in COLUMNS[place : place + 2]:
            chip = lax.rem(xl + dxl, 2) * ny + lax.rem(y + dy, ny)
            block = scratch[:, pl.ds(pl.multiple_of(chip * wide, 128), wide)]
            first, second = block[:, :rows], block[:, rows:]
            mine.append(jnp.where(low, first, second))
            other.append(jnp.where(low, second, first))
        here = slice(place * rows, (place + 2) * rows)
        mine_ref[:, here] = jnp.concatenate(mine, axis=1)
        other_ref[:, here] = jnp.concatenate(other, axis=1)


def modulate(states, t_index, mod_table, coef, rows):
    _, tokens, width = states.shape
    half = jax.ShapeDtypeStruct((tokens, width // 2), BF16)
    return pl.pallas_call(
        functools.partial(modulate_kernel, rows),
        out_shape=(half, half, jax.ShapeDtypeStruct((1, width), F32)),
        grid_spec=pltpu.PrefetchScalarGridSpec(
            num_scalar_prefetch=1,
            grid=(1,),
            in_specs=[
                pl.BlockSpec((1, tokens, width), lambda i, t: (0, 0, 0)),
                pl.BlockSpec((3, 8, width), lambda i, t: (0, t[0] // 8, 0)),
                pl.BlockSpec(memory_space=pltpu.SMEM),
            ],
            out_specs=[
                pl.BlockSpec((tokens, width // 2), lambda i, t: (0, 0)),
                pl.BlockSpec((tokens, width // 2), lambda i, t: (0, 0)),
                pl.BlockSpec((1, width), lambda i, t: (0, 0)),
            ],
            scratch_shapes=[pltpu.VMEM((tokens, width), BF16)],
        ),
        compiler_params=pltpu.CompilerParams(vmem_limit_bytes=VMEM_BYTES),
        cost_estimate=pl.CostEstimate(flops=1000, bytes_accessed=1000, transcendentals=0),
    )(t_index, states, jnp.transpose(mod_table, (1, 0, 2)), coef)


def normed(x):
    return (x * lax.rsqrt(jnp.mean(x * x, axis=-1, keepdims=True) + 1e-06)).astype(BF16)


def attend(query, keys, values):
    scores = lax.dot_general(query, keys, (((1,), (1,)), ((), ())), preferred_element_type=F32)
    expo = jnp.exp(scores * HEAD_DIM ** (-0.5))
    total = jnp.sum(expo, axis=-1, keepdims=True)
    return (
        jnp.dot(expo.astype(BF16), values, preferred_element_type=F32) * (1.0 / total)
    ).astype(BF16)


def first_kernel(head, q, qb, k, kb, v, vb, query_ref, keys_ref, values_ref, out_ref):
    half = v.shape[0] // 2
    for h in range(v.shape[1] // HEAD_DIM):
        at = slice(h * HEAD_DIM, (h + 1) * HEAD_DIM)
        query = normed(q[:, at] + qb[:, at].astype(F32))
        keys = normed(k[:, at] + kb[:, at].astype(F32))
        values = (v[:, at] + vb[:, at].astype(F32)).astype(BF16)
        query_ref[:, at], keys_ref[:, at], values_ref[:, at] = query, keys, values
        out_ref[:, at] = attend(query[half : half + head], keys, values)


def second_kernel(head, query_ref, keys_ref, values_ref, out_ref):
    half = query_ref.shape[0] // 2
    for h in range(query_ref.shape[1] // HEAD_DIM):
        at = slice(h * HEAD_DIM, (h + 1) * HEAD_DIM)
        query = jnp.concatenate([query_ref[:half, at], query_ref[half + head :, at]], axis=0)
        out_ref[:, at] = attend(query, keys_ref[:, at], values_ref[:, at])


def last_kernel(matrices, f0, f1, far, extra, *refs):
    rows, count, columns = far.shape[1], f0.shape[0], far.shape[2]
    half, each = count // 2, len(matrices)
    mates = [far[3 + j] if j < 2 else extra[...] for j in matrices]
    weights = [jnp.concatenate([far[j], mate], axis=0) for j, mate in zip(matrices, mates)]
    weight = jnp.concatenate(weights, axis=1)
    for dx, f in enumerate((f0, f1)):
        products = jnp.dot(f[:, 6 * rows :], weight, preferred_element_type=F32)
        for i in range(each):
            own_ref, mate_ref = refs[2 * each + 2 * i : 2 * each + 2 * i + 2]
            total = refs[2 * i + dx][...] + products[:, i * columns : (i + 1) * columns]
            own_ref[dx * half : (dx + 1) * half] = total[:half]
            mate_ref[dx * half : (dx + 1) * half] = total[half:].astype(BF16)


def local_call(kernel, operands, shapes, flops):
    whole = pl.BlockSpec(memory_space=pltpu.VMEM)
    return pl.pallas_call(
        kernel,
        out_shape=[jax.ShapeDtypeStruct(*shape) for shape in shapes],
        in_specs=[whole] * len(operands),
        out_specs=[whole] * len(shapes),
        compiler_params=pltpu.CompilerParams(vmem_limit_bytes=24 * 1024 * 1024),
        cost_estimate=pl.CostEstimate(flops=flops, bytes_accessed=1000, transcendentals=0),
    )(*operands)


def on_device(states, start, t_index, coef, mod_table, wqkv, wo):
    tokens, width = states.shape[1:]
    rows = wqkv.shape[1]
    half, short = rows // 2, tokens // 2

    own = wqkv
    a1, b1 = send(own, "y", -1), send(own, "y", 1)
    p = send(own[:2], "xl", 1)

    mine, other, gate_row = modulate(states, t_index, mod_table, coef, rows)
    pair = jnp.stack([mine, send(other, "core", 1)])

    za, zb = send(pair, "z", -1), send(pair, "z", 1)
    across = send(after(pair, p), "xh", 1)
    near = after(p, za, zb)
    pa, pb = send(near, "y", -1), send(near, "y", 1)
    zfa = send(after(za[:, :short], a1, b1), "z", -1)
    zfb = send(after(zb[:, short:], a1, b1), "z", 1)

    xv = send(after(jnp.stack([own[2], a1[2], b1[2]]), across), "xl", 1)
    distant = after(across, zfa, zfb)
    xa, xb = send(distant, "z", -1), send(distant, "z", 1)

    fa = send(jnp.concatenate([a1[:, :half], pa[:, :half]], axis=0), "y", -1)
    fb = send(jnp.concatenate([b1[:, half:], pb[:, half:]], axis=0), "y", 1)
    xfa = send(after(xa[:, :short], xb), "z", -1)
    xfb = send(after(xb[:, short:], xa), "z", 1)
    vfa = send(after(xv[1, :half], xfa, xfb), "y", -1)
    vfb = send(after(xv[2, half:], xfa, xfb), "y", 1)
    far = jnp.concatenate([fa, fb], axis=1)
    vfar = jnp.concatenate([vfa, vfb], axis=0)

    features = []
    for near, above, below, ends in ((pair, za, zb, (zfa, zfb)), (across, xa, xb, (xfa, xfb))):
        rowed = jnp.concatenate([*ends, above, below, near], axis=1)
        features.append(rowed.reshape(2 * rowed.shape[1], -1))
    count = features[0].shape[0]

    def product(begin, blocks):
        stop = begin + len(blocks) * rows
        weight = jnp.concatenate(blocks, axis=0)
        return [jnp.dot(f[:, begin:stop], weight, preferred_element_type=F32) for f in features]

    def plus(sofar, more):
        return [a + b for a, b in zip(sofar, more)]

    held = lax.optimization_barrier
    begun = [[held(x) for x in product(0, [own[j], a1[j], p[j], pa[j], b1[j], pb[j]])] for j in range(2)]
    begun.append([held(x) for x in product(0, [own[2], a1[2]])])
    begun[2] = [held(x) for x in plus(begun[2], product(2 * rows, [xv[0], xv[1], b1[2], xv[2]]))]
    columns = wqkv.shape[2]
    one = (count, columns)
    q, q_mates, k, k_mates = local_call(
        functools.partial(last_kernel, (0, 1)), (*features, far, far, *begun[0], *begun[1]),
        [(one, F32), (one, BF16)] * 2, 1000,
    )
    v, v_mates = local_call(
        functools.partial(last_kernel, (2,)), (*features, far, vfar, *begun[2]),
        [(one, F32), (one, BF16)], 8 * count * rows * columns,
    )
    parts = (q, send(q_mates, "core", 1), k, send(k_mates, "core", 1), v, send(v_mates, "core", 1))

    cut, head = width // 2, 3 * tokens
    query, keys, values, attended = local_call(
        functools.partial(first_kernel, head), parts, [(one, BF16)] * 3 + [((head, columns), BF16)],
        4 * head * count * columns,
    )
    first = jnp.dot(attended, wo, preferred_element_type=F32).astype(BF16)
    far1, above1, below1 = (first[i * tokens : (i + 1) * tokens] for i in range(3))
    up1, down1 = send(above1, "z", 1), send(below1, "z", -1)
    quarter = cut // 2
    joins = [send(far1[:, :quarter], "xh", 1), send(far1[:, quarter:], "xh", 1)]
    (attended,) = local_call(
        functools.partial(second_kernel, head), (after(query, joins[0]), keys, values),
        [((count - head, columns), BF16)], 4 * (count - head) * count * columns,
    )
    rest = jnp.dot(attended, wo, preferred_element_type=F32)
    far0, above0, below0, near0, near1 = (rest[i * tokens : (i + 1) * tokens] for i in range(5))
    far0 = (far0 + jnp.concatenate(joins, axis=1).astype(F32)).astype(BF16)
    up, down = send(far0[:, :cut], "z", 1), send(far0[:, cut:], "z", -1)
    free = (
        send(after(above0[:, cut:].astype(BF16), up1, down1), "z", 1),
        send(after(below0[:, :cut].astype(BF16), up1, down1), "z", -1),
    )
    near1 = after(near1, far0)
    there = send((near1 + up1.astype(F32) + down1.astype(F32)).astype(BF16), "xh", 1)
    bound = (
        send((above0[:, :cut] + up.astype(F32)).astype(BF16), "z", 1),
        send((below0[:, cut:] + down.astype(F32)).astype(BF16), "z", -1),
    )
    output = (
        near0
        + jnp.concatenate([bound[0], free[0]], axis=1).astype(F32)
        + jnp.concatenate([free[1], bound[1]], axis=1).astype(F32)
        + there.astype(F32)
    )
    term = (gate_row * output).astype(BF16)
    steps = lax.axis_size(TM)
    by_step = lax.all_to_all(term.reshape(steps, tokens // steps, width), TM, 0, 0)
    total = jnp.cumsum(by_step.astype(F32), axis=0).astype(BF16)
    total = lax.all_to_all(total, TM, 0, 0).reshape(tokens, width)
    return (start + total.astype(F32))[None]


def solution(mesh):
    wide = Mesh(mesh.devices.reshape(2, 4, 2, 2, 4), TM + SEQ)
    placed = (
        P(TM, SEQ, None),
        P(SEQ, None),
        P(TM),
        P(),
        P(),
        P(None, TM, SEQ),
        P(SEQ, None),
    )
    return jax.shard_map(
        on_device, mesh=wide, in_specs=placed, out_specs=P(TM, SEQ, None), check_vma=False
    )
```

```python
import functools

import jax
import jax.numpy as jnp
from jax import lax
from jax.experimental import pallas as pl
from jax.experimental.pallas import tpu as pltpu
from jax.sharding import Mesh, PartitionSpec as P

HEAD_DIM = 128
TM = ("xl", "y", "core")
SEQ = ("xh", "z")
F32, BF16 = jnp.float32, jnp.bfloat16
VMEM_BYTES = 60 * 1024 * 1024
COLUMNS = [(0, 0), (1, 0), (0, 1), (1, 1), (3, 0), (3, 1), (2, 0), (2, 1)]
BLOCKS = [2, 1, 3, 0]


def send(array, axis, shift):
    size = lax.axis_size(axis)
    return lax.ppermute(array, axis, [(i, (i + shift) % size) for i in range(size)])


def after(array, *others):
    return lax.optimization_barrier((array,) + others)[0]


def add(a, b):
    return (a.astype(F32) + b.astype(F32)).astype(BF16)


def modulate_kernel(rows, t_ref, state_ref, mod_ref, coef_ref, mine_ref, other_ref, gate_ref, scratch):
    state = state_ref[0]
    line = pl.ds(lax.rem(t_ref[0], 8), 1)
    shift_row, scale_row = mod_ref[0, line, :], mod_ref[1, line, :]
    gate_ref[...] = mod_ref[2, line, :] * coef_ref[t_ref[0]]
    center = jnp.mean(state, axis=-1, keepdims=True)
    moved = state - center
    spread = jnp.mean(moved * moved, axis=-1, keepdims=True)
    scratch[...] = moved * lax.rsqrt(spread + 1e-06) * (1.0 + scale_row) + shift_row
    xl, y, core = (lax.axis_index(a) for a in TM)
    ny, wide = 4, 2 * rows
    low = core == 0
    for place in range(0, len(COLUMNS), 2):
        mine, other = [], []
        for dy, dxl in COLUMNS[place : place + 2]:
            chip = lax.rem(xl + dxl, 2) * ny + lax.rem(y + dy, ny)
            block = scratch[:, pl.ds(pl.multiple_of(chip * wide, 128), wide)]
            first, second = block[:, :rows], block[:, rows:]
            mine.append(jnp.where(low, first, second))
            other.append(jnp.where(low, second, first))
        here = slice(place * rows, (place + 2) * rows)
        mine_ref[:, here] = jnp.concatenate(mine, axis=1).astype(BF16)
        other_ref[:, here] = jnp.concatenate(other, axis=1).astype(BF16)


def modulate(states, t_index, mod_table, coef, rows):
    _, tokens, width = states.shape
    half = jax.ShapeDtypeStruct((tokens, width // 2), BF16)
    return pl.pallas_call(
        functools.partial(modulate_kernel, rows),
        out_shape=(half, half, jax.ShapeDtypeStruct((1, width), F32)),
        grid_spec=pltpu.PrefetchScalarGridSpec(
            num_scalar_prefetch=1,
            grid=(1,),
            in_specs=[
                pl.BlockSpec((1, tokens, width), lambda i, t: (0, 0, 0)),
                pl.BlockSpec((3, 8, width), lambda i, t: (0, t[0] // 8, 0)),
                pl.BlockSpec(memory_space=pltpu.SMEM),
            ],
            out_specs=[
                pl.BlockSpec((tokens, width // 2), lambda i, t: (0, 0)),
                pl.BlockSpec((tokens, width // 2), lambda i, t: (0, 0)),
                pl.BlockSpec((1, width), lambda i, t: (0, 0)),
            ],
            scratch_shapes=[pltpu.VMEM((tokens, width), F32)],
        ),
        compiler_params=pltpu.CompilerParams(vmem_limit_bytes=VMEM_BYTES),
        cost_estimate=pl.CostEstimate(flops=1000, bytes_accessed=1000, transcendentals=0),
    )(t_index, states, jnp.transpose(mod_table, (1, 0, 2)), coef)


def normed(x):
    return (x * lax.rsqrt(jnp.mean(x * x, axis=-1, keepdims=True) + 1e-06)).astype(BF16)


def attend(query, keys, values):
    scores = lax.dot_general(query, keys, (((1,), (1,)), ((), ())), preferred_element_type=F32)
    expo = jnp.exp2(scores * (HEAD_DIM ** (-0.5) * 1.4426950408889634))
    total = jnp.sum(expo, axis=-1, keepdims=True)
    return (
        jnp.dot(expo.astype(BF16), values, preferred_element_type=F32) * (1.0 / total)
    ).astype(BF16)


def first_kernel(head, q, qb, k, kb, v, vb, query_ref, keys_ref, values_ref, out_ref):
    half = v.shape[0] // 2
    for h in range(v.shape[1] // HEAD_DIM):
        at = slice(h * HEAD_DIM, (h + 1) * HEAD_DIM)
        query = normed(q[:, at] + qb[:, at].astype(F32))
        keys = normed(k[:, at] + kb[:, at].astype(F32))
        values = (v[:, at] + vb[:, at].astype(F32)).astype(BF16)
        query_ref[:, at], keys_ref[:, at], values_ref[:, at] = query, keys, values
        out_ref[:, at] = attend(query[half : half + head], keys, values)


def second_kernel(head, query_ref, keys_ref, values_ref, out_ref):
    half = query_ref.shape[0] // 2
    for h in range(query_ref.shape[1] // HEAD_DIM):
        at = slice(h * HEAD_DIM, (h + 1) * HEAD_DIM)
        query = jnp.concatenate([query_ref[:half, at], query_ref[half + head :, at]], axis=0)
        out_ref[:, at] = attend(query, keys_ref[:, at], values_ref[:, at])


def last_kernel(matrices, f0, f1, far, extra, *refs):
    rows, count = far.shape[1], f0.shape[0]
    half, each = count // 2, len(matrices)
    for i, j in enumerate(matrices):
        mate = far[3 + j] if j < 2 else extra[...]
        weight = jnp.concatenate([far[j], mate], axis=0)
        own_ref, mate_ref = refs[2 * each + 2 * i : 2 * each + 2 * i + 2]
        for dx, f in enumerate((f0, f1)):
            total = refs[2 * i + dx][...] + jnp.dot(
                f[:, 6 * rows :], weight, preferred_element_type=F32
            )
            own_ref[dx * half : (dx + 1) * half] = total[:half]
            mate_ref[dx * half : (dx + 1) * half] = total[half:].astype(BF16)


def local_call(kernel, operands, shapes, flops):
    whole = pl.BlockSpec(memory_space=pltpu.VMEM)
    return pl.pallas_call(
        kernel,
        out_shape=[jax.ShapeDtypeStruct(*shape) for shape in shapes],
        in_specs=[whole] * len(operands),
        out_specs=[whole] * len(shapes),
        compiler_params=pltpu.CompilerParams(vmem_limit_bytes=24 * 1024 * 1024),
        cost_estimate=pl.CostEstimate(flops=flops, bytes_accessed=1000, transcendentals=0),
    )(*operands)


def on_device(states, start, t_index, coef, mod_table, wqkv, wo):
    tokens, width = states.shape[1:]
    rows = wqkv.shape[1]
    half, short = rows // 2, tokens // 2

    own = wqkv
    a1, b1 = send(own, "y", -1), send(own, "y", 1)
    p = send(own[:2], "xl", 1)

    mine, other, gate_row = modulate(states, t_index, mod_table, coef, rows)
    pair = jnp.stack([mine, send(other, "core", 1)])

    za, zb = send(pair, "z", -1), send(pair, "z", 1)
    across = send(after(pair, p), "xh", 1)
    near = after(p, za, zb)
    pa, pb = send(near, "y", -1), send(near, "y", 1)
    zfa = send(after(za[:, :short], a1, b1), "z", -1)
    zfb = send(after(zb[:, short:], a1, b1), "z", 1)

    xv = send(after(jnp.stack([own[2], a1[2], b1[2]]), across), "xl", 1)
    distant = after(across, zfa, zfb)
    xa, xb = send(distant, "z", -1), send(distant, "z", 1)

    fa = send(jnp.concatenate([a1[:, :half], pa[:, :half]], axis=0), "y", -1)
    fb = send(jnp.concatenate([b1[:, half:], pb[:, half:]], axis=0), "y", 1)
    xfa = send(after(xa[:, :short], xb), "z", -1)
    xfb = send(after(xb[:, short:], xa), "z", 1)
    vfa = send(after(xv[1, :half], xfa, xfb), "y", -1)
    vfb = send(after(xv[2, half:], xfa, xfb), "y", 1)
    far = jnp.concatenate([fa, fb], axis=1)
    vfar = jnp.concatenate([vfa, vfb], axis=0)

    features = []
    for near, above, below, ends in ((pair, za, zb, (zfa, zfb)), (across, xa, xb, (xfa, xfb))):
        rowed = jnp.concatenate([*ends, above, below, near], axis=1)
        features.append(rowed.reshape(2 * rowed.shape[1], -1))
    count = features[0].shape[0]

    def product(begin, blocks):
        stop = begin + len(blocks) * rows
        weight = jnp.concatenate(blocks, axis=0)
        return [jnp.dot(f[:, begin:stop], weight, preferred_element_type=F32) for f in features]

    def plus(sofar, more):
        return [a + b for a, b in zip(sofar, more)]

    held = lax.optimization_barrier
    begun = [[held(x) for x in product(0, [own[j], a1[j], p[j], pa[j], b1[j], pb[j]])] for j in range(2)]
    begun.append([held(x) for x in product(0, [own[2], a1[2]])])
    begun[2] = [held(x) for x in plus(begun[2], product(2 * rows, [xv[0], xv[1], b1[2], xv[2]]))]
    columns = wqkv.shape[2]
    one = (count, columns)
    q, q_mates, k, k_mates = local_call(
        functools.partial(last_kernel, (0, 1)), (*features, far, far, *begun[0], *begun[1]),
        [(one, F32), (one, BF16)] * 2, 1000,
    )
    v, v_mates = local_call(
        functools.partial(last_kernel, (2,)), (*features, far, vfar, *begun[2]),
        [(one, F32), (one, BF16)], 8 * count * rows * columns,
    )
    parts = (q, send(q_mates, "core", 1), k, send(k_mates, "core", 1), v, send(v_mates, "core", 1))

    cut, head = width // 2, 3 * tokens
    query, keys, values, attended = local_call(
        functools.partial(first_kernel, head), parts, [(one, BF16)] * 3 + [((head, columns), BF16)],
        4 * head * count * columns,
    )
    first = jnp.dot(attended, wo, preferred_element_type=F32).astype(BF16)
    far1, above1, below1 = (first[i * tokens : (i + 1) * tokens] for i in range(3))
    up1, down1 = send(above1, "z", 1), send(below1, "z", -1)
    quarter = cut // 2
    joins = [send(far1[:, :quarter], "xh", 1), send(far1[:, quarter:], "xh", 1)]
    (attended,) = local_call(
        functools.partial(second_kernel, head), (after(query, joins[0]), keys, values),
        [((count - head, columns), BF16)], 4 * (count - head) * count * columns,
    )
    rest = jnp.dot(attended, wo, preferred_element_type=F32)
    far0, above0, below0, near0, near1 = (rest[i * tokens : (i + 1) * tokens] for i in range(5))
    far0 = (far0 + jnp.concatenate(joins, axis=1).astype(F32)).astype(BF16)
    up, down = send(far0[:, :cut], "z", 1), send(far0[:, cut:], "z", -1)
    free = (
        send(after(above0[:, cut:].astype(BF16), up1, down1), "z", 1),
        send(after(below0[:, :cut].astype(BF16), up1, down1), "z", -1),
    )
    near1 = after(near1, far0)
    there = send((near1 + up1.astype(F32) + down1.astype(F32)).astype(BF16), "xh", 1)
    bound = (
        send((above0[:, :cut] + up.astype(F32)).astype(BF16), "z", 1),
        send((below0[:, cut:] + down.astype(F32)).astype(BF16), "z", -1),
    )
    output = (
        near0
        + jnp.concatenate([bound[0], free[0]], axis=1).astype(F32)
        + jnp.concatenate([free[1], bound[1]], axis=1).astype(F32)
        + there.astype(F32)
    )
    term = (gate_row * output).astype(BF16)
    steps = lax.axis_size(TM)
    by_step = lax.all_to_all(term.reshape(steps, tokens // steps, width), TM, 0, 0)
    total = jnp.cumsum(by_step.astype(F32), axis=0).astype(BF16)
    total = lax.all_to_all(total, TM, 0, 0).reshape(tokens, width)
    return (start + total.astype(F32))[None]


def solution(mesh):
    wide = Mesh(mesh.devices.reshape(2, 4, 2, 2, 4), TM + SEQ)
    placed = (
        P(TM, SEQ, None),
        P(SEQ, None),
        P(TM),
        P(),
        P(),
        P(None, TM, SEQ),
        P(SEQ, None),
    )
    return jax.shard_map(
        on_device, mesh=wide, in_specs=placed, out_specs=P(TM, SEQ, None), check_vma=False
    )
```
